32 devices in a mesh: node: 8 (over y, x, core), group: 4 (over z).
Axes of the slice: x: 2, y: 2, z: 4, core: 2. Of those that a mesh axis runs over, the one named last changes fastest.
Arguments:
- tokens: bfloat16 [1024, 3584], P('node', 'group'), may hold values from -10 to 10
- node_routes: int32 [1024, 4], P('node'), may hold values from 0 to 7, all different within a row; in each aligned block of 128 rows (0 to 127, 128 to 255, ...) at most 128 rows name the same one
- combine: int32 [1024, 8], P('node'), may hold values from 64 to 256
- w_gate: bfloat16 [3584, 16384], P(None, ('node', 'group')), may hold values from -0.09375 to 0.09375
- w_up: bfloat16 [3584, 16384], P(None, ('node', 'group')), may hold values from -0.09375 to 0.09375
- w_down: bfloat16 [3584, 16384], P('group', 'node'), may hold values from -0.1875 to 0.1875
Outputs:
- moe_out: bfloat16 [1024, 3584], P('node', 'group')
The draws below stay inside these ranges and needn't reach their ends.
Inputs may be any that keep to these rules, and one draw needn't show every extreme that they name: `node_routes`: each token names 4 different nodes. Among the 128 tokens of one node (rows n * 128 to (n + 1) * 128 - 1) no node is named by more than 128 tokens, a bound that some block reaches of them.
All inputs are finite; a program needn't handle non-finite values.
Results may differ from the reference program's by a relative error of at most 0.0057.
Values may be sent and summed in bfloat16 or wider, within the bound.
A program may use at most 64 MiB of HBM per device.

```python
import math
import jax
import jax.numpy as jnp
import numpy as np
from jax import lax

D = 3584
F = 1024
EXP_NODE = 2
NODES_TOK = 4
TOK_NODE = 128
CAP = 128
TOPK = 8
EXPERTS = 16
TOKENS = 1024
N_NODE = 8


def plant(entries, stream_key, low, high):
    index_at = [jax.random.randint(jax.random.fold_in(stream_key, axis), (), 0, length) for axis, length in enumerate(entries.shape)]
    widest = entries.shape.index(max(entries.shape))
    next_to = index_at[:widest] + [(index_at[widest] + 1) % entries.shape[widest]] + index_at[widest + 1:]
    return entries.at[tuple(index_at)].set(low).at[tuple(next_to)].set(high)


def level_of(key, extent, cuts, smallest, largest):
    level, own = 1.0, jax.random.fold_in(key, 6)
    for dim, blocks in cuts:
        steps = jnp.exp(jax.random.uniform(jax.random.fold_in(own, dim), (blocks,), jnp.float32, smallest / len(cuts), largest / len(cuts)))
        level = level * jnp.repeat(steps, extent[dim] // blocks).reshape([-1 if axis == dim else 1 for axis in range(len(extent))])
    return level


def assign_block(rng, own, number, rows, count, top, limit, skew):
    ranking = jax.random.permutation(rng, count)
    heavy_load, common = load_shares(count, rows * top, limit, skew, True), load_shares(count, rows * top, limit, skew, False)
    places = jnp.arange(count)

    def named(tallies, rotation):
        used = int((tallies > 0).sum())
        fixed = max(1, used // 4)
        shifted = fixed + (places - fixed + rotation * (used - fixed)) % max(1, count - fixed)
        return jnp.zeros((count,), jnp.int32).at[ranking[jnp.where(places < fixed, places, shifted)]].set(jnp.asarray(tallies, jnp.int32))

    tallies = jnp.where(number % 4 == 0, named(heavy_load, number // 4), named(common, number - number // 4 - 1))
    mixed = jax.random.permutation(jax.random.fold_in(own, 3), count)
    source_of, taker = mixed[0:count // 2 * 2:2], mixed[1:count // 2 * 2:2]
    slack = jnp.minimum(tallies[source_of] - 1, limit - tallies[taker]) // 2
    slack = jnp.where((source_of == ranking[0]) | (taker == ranking[0]) | (tallies[taker] == 0), 0, jnp.maximum(slack, 0))
    shifted = jax.random.randint(jax.random.fold_in(own, 4), (count // 2,), 0, 1 << 20) % (slack + 1)
    tallies = tallies.at[source_of].add(-shifted).at[taker].add(shifted)
    labels = jnp.searchsorted(jnp.cumsum(tallies), jnp.arange(rows * top), side="right").astype(jnp.int32)
    listing = labels.reshape(top, rows).T
    listing = listing[jax.random.permutation(jax.random.fold_in(own, 1), rows)]
    rotation = jax.random.randint(jax.random.fold_in(own, 2), (rows, 1), 0, top)
    return jnp.take_along_axis(listing, (jnp.arange(top)[None, :] + rotation) % top, axis=1)


def load_shares(amount, total, bound, lean, full):
    portions = [(1 << 20) // math.isqrt(grade ** lean) + 1 for grade in range(1, amount + 1)]
    largest = bound if full else min(bound, max(-(-total // amount), total * portions[0] // sum(portions)))
    least = 1 if total - largest >= amount - 1 else 0
    counts, rest = [largest] + [least] * (amount - 1), total - largest - least * (amount - 1)
    while rest > 0:
        movable = [i for i in range(1, amount) if counts[i] < largest] or [i for i in range(1, amount) if counts[i] < bound]
        whole, budget = sum([portions[i] for i in movable]), rest
        for i in movable:
            addition = min(bound - counts[i], max(1, budget * portions[i] // whole), rest)
            counts[i] = counts[i] + addition
            rest = rest - addition
    return np.array(counts)


def centred(key, shape, width, reach, cuts=(), held_as=jnp.bfloat16):
    entries = jax.random.normal(key, shape, jnp.float32) * width
    if len(cuts) > 0:
        entries = level_of(key, shape, cuts, -0.22, 0.18) * entries
    return jnp.clip(entries, min=-reach, max=reach).astype(held_as)


def setup_inputs(seed: int = 0) -> dict:
    arg_keys = jax.random.split(jax.random.key(seed), 7)
    tokens = centred(arg_keys[0], (TOKENS, D), 2.0, 10.0, ((0, 8), (1, 4)))
    node_routes_keys = jax.random.split(jax.random.fold_in(arg_keys[1], 1), TOKENS // TOK_NODE)
    node_routes_turns = jax.random.permutation(jax.random.fold_in(arg_keys[1], 3), TOKENS // TOK_NODE)
    node_routes = jax.vmap(lambda own, number: assign_block(jax.random.fold_in(arg_keys[1], 2), own, number, TOK_NODE, N_NODE, NODES_TOK, CAP, 2))(node_routes_keys, node_routes_turns).reshape((TOKENS, NODES_TOK))
    combine = plant(jax.random.randint(arg_keys[2], (TOKENS, TOPK), 64, 257), jax.random.fold_in(arg_keys[2], 1), 64, 256).astype(jnp.int32)
    w_gate = centred(arg_keys[3], (D, EXPERTS * F), D ** -0.5, 0.09375, ((1, 32),))
    w_up = centred(arg_keys[4], (D, EXPERTS * F), D ** -0.5, 0.09375, ((1, 32),))
    w_down = centred(arg_keys[5], (D, EXPERTS * F), F ** -0.5, 0.1875, ((0, 4), (1, 8)))
    return {"tokens": tokens, "node_routes": node_routes, "combine": combine, "w_gate": w_gate, "w_up": w_up, "w_down": w_down}


def reference(tokens, node_routes, combine, w_gate, w_up, w_down):
    node_width = EXP_NODE * F
    rows_node = N_NODE * CAP
    targets = jnp.arange(N_NODE, dtype=jnp.int32)
    node_hits = (node_routes[:, :, None] == targets[None, None, :])
    hit_float = node_hits.astype(jnp.float32)
    member = jnp.sum(node_hits.astype(jnp.int32), axis=1).reshape(N_NODE, TOK_NODE, N_NODE)
    slot_rank = jnp.cumsum(member, axis=1) - member
    slot_numbers = jnp.arange(CAP, dtype=jnp.int32)
    placed = member[..., None] * (slot_rank[..., None] == slot_numbers).astype(jnp.int32)
    token_ids = jnp.arange(TOKENS, dtype=jnp.int32).reshape(N_NODE, TOK_NODE)
    slot_table = jnp.sum(placed * token_ids[:, :, None, None], axis=1)
    slot_table = jnp.transpose(slot_table, (1, 0, 2)).astype(jnp.int32)
    pair_weights = combine.reshape(TOKENS, NODES_TOK, EXP_NODE).astype(jnp.float32) / 1024.0
    node_pair = jnp.einsum("tjm,tjk->tmk", hit_float, pair_weights)
    node_pair = node_pair.reshape(N_NODE, TOK_NODE, N_NODE, EXP_NODE)
    slot_weights = jnp.einsum("stdc,stdk->dsck", placed.astype(jnp.float32), node_pair)

    def one_node(node_index):
        slot_ids = lax.dynamic_index_in_dim(slot_table, node_index, 0, keepdims=False).reshape(rows_node)
        slot_scale = lax.dynamic_index_in_dim(slot_weights, node_index, 0, keepdims=False).reshape(rows_node, EXP_NODE)
        slot_rows = jnp.take(tokens, slot_ids, axis=0)
        column_start = (node_index * node_width).astype(jnp.int32)
        gate_cols = lax.dynamic_slice_in_dim(w_gate, column_start, node_width, 1)
        up_cols = lax.dynamic_slice_in_dim(w_up, column_start, node_width, 1)
        down_cols = lax.dynamic_slice_in_dim(w_down, column_start, node_width, 1)
        gate_acts = jnp.dot(slot_rows, gate_cols, preferred_element_type=jnp.float32)
        up_acts = jnp.dot(slot_rows, up_cols, preferred_element_type=jnp.float32)
        expanded = jnp.repeat(slot_scale, F, axis=1)
        hidden = (expanded * jax.nn.silu(gate_acts) * up_acts).astype(jnp.bfloat16)
        return jnp.dot(hidden, down_cols.T, preferred_element_type=jnp.float32).astype(jnp.bfloat16)

    node_parts = lax.map(one_node, jnp.arange(N_NODE, dtype=jnp.int32))
    summed = jnp.zeros((TOKENS, D), jnp.float32).at[slot_table.reshape(-1)].add(node_parts.reshape(-1, D).astype(jnp.float32))
    return summed.astype(jnp.bfloat16)
```

```python
import jax
import jax.numpy as jnp
from jax import lax
from jax.sharding import PartitionSpec as P

F = 1024
EXP_NODE = 2


def routed_shards(tokens, node_routes, combine, w_gate, w_up, w_down):
    node_count = lax.axis_size("node")
    tok_count = tokens.shape[0]
    col_width = tokens.shape[1]
    hid_dev = w_gate.shape[1]
    slots = 2 * tok_count * node_routes.shape[1] // node_count
    row_total = node_count * slots
    targets = jnp.arange(node_count, dtype=jnp.int32)
    node_hits = (node_routes[:, :, None] == targets[None, None, :]).astype(jnp.float32)
    member = jnp.sum(node_hits, axis=1)
    slot_rank = jnp.cumsum(member, axis=0) - member
    slot_numbers = jnp.arange(slots, dtype=jnp.float32)
    placed = member[:, :, None] * (slot_rank[:, :, None] == slot_numbers).astype(jnp.float32)
    pair_weights = combine.reshape(tok_count, -1, EXP_NODE).astype(jnp.float32) / 1024.0
    node_pair = jnp.einsum("tjm,tjk->tmk", node_hits, pair_weights)
    slot_weights = jnp.einsum("tmc,tmk->mck", placed, node_pair).astype(jnp.bfloat16)
    placed_low = placed.astype(jnp.bfloat16)
    send_rows = jnp.einsum(
        "tmc,td->mcd", placed_low, tokens, preferred_element_type=jnp.float32
    ).astype(jnp.bfloat16)
    send_rows = send_rows.reshape(node_count, slots * col_width)
    got_rows, got_weights = (
        lax.all_to_all(send_rows, "node", split_axis=0, concat_axis=0, tiled=True),
        lax.all_to_all(slot_weights, "node", split_axis=0, concat_axis=0, tiled=True),
    )
    node_rows = got_rows.reshape(row_total, col_width)
    weight_rows = got_weights.reshape(row_total, EXP_NODE).astype(jnp.float32)
    local_expert = lax.axis_index("group") * hid_dev // F
    expert_pick = (jnp.arange(EXP_NODE, dtype=jnp.int32) == local_expert).astype(jnp.float32)
    row_scale = jnp.sum(weight_rows * expert_pick[None, :], axis=1)
    whole_rows = lax.all_gather(node_rows, "group", axis=1, tiled=True)
    gate_acts = jnp.dot(whole_rows, w_gate, preferred_element_type=jnp.float32)
    up_acts = jnp.dot(whole_rows, w_up, preferred_element_type=jnp.float32)
    hidden = (row_scale[:, None] * jax.nn.silu(gate_acts) * up_acts).astype(jnp.bfloat16)
    contract = (((1,), (1,)), ((), ()))
    all_hidden = lax.all_gather(hidden, "group", axis=1, tiled=True)
    out_back = lax.dot_general(w_down, all_hidden, contract, preferred_element_type=jnp.float32)
    out_back = out_back.astype(jnp.bfloat16)
    returned = lax.all_to_all(out_back, "node", split_axis=1, concat_axis=1, tiled=True)
    mixed_out = lax.dot_general(
        placed_low.reshape(tok_count, row_total),
        returned,
        contract,
        preferred_element_type=jnp.float32,
    )
    return mixed_out.astype(jnp.bfloat16)


def pair_scales(node_routes, combine):
    node_count = lax.axis_size("node")
    targets = jnp.arange(node_count, dtype=jnp.int32)
    hits = (node_routes[:, :, None] == targets[None, None, :]).astype(jnp.float32)
    pairs = combine.reshape(combine.shape[0], -1, EXP_NODE).astype(jnp.float32) / 1024.0
    return jnp.einsum("tjm,tjk->tmk", hits, pairs).reshape(combine.shape[0], -1)


def dense_shards(tokens, node_routes, combine, w_gate, w_up, w_down):
    hid_dev = w_gate.shape[1]
    scales = pair_scales(node_routes, combine).astype(jnp.bfloat16)
    all_scales = lax.all_gather(scales, "node", axis=0, tiled=True)
    column = lax.all_gather(tokens, "group", axis=1, tiled=True)
    rows = lax.all_gather(column, "node", axis=0, tiled=True)
    expert = EXP_NODE * lax.axis_index("node") + lax.axis_index("group") * hid_dev // F
    row_scale = lax.dynamic_slice_in_dim(all_scales, expert, 1, 1).astype(jnp.float32)
    gate_acts = jnp.dot(rows, w_gate, preferred_element_type=jnp.float32)
    up_acts = jnp.dot(rows, w_up, preferred_element_type=jnp.float32)
    hidden = (row_scale * jax.nn.silu(gate_acts) * up_acts).astype(jnp.bfloat16)
    all_hidden = lax.all_gather(hidden, "group", axis=1, tiled=True)
    contract = (((1,), (1,)), ((), ()))
    part = lax.dot_general(all_hidden, w_down, contract, preferred_element_type=jnp.float32)
    return lax.psum_scatter(part.astype(jnp.bfloat16), "node", scatter_dimension=0, tiled=True)


def shards(tokens, node_routes, *rest):
    slots = 2 * tokens.shape[0] * node_routes.shape[1] // lax.axis_size("node")
    if slots == tokens.shape[0]:
        return dense_shards(tokens, node_routes, *rest)
    return routed_shards(tokens, node_routes, *rest)


def solution(mesh):
    in_specs = (
        P("node", "group"),
        P("node", None),
        P("node", None),
        P(None, ("node", "group")),
        P(None, ("node", "group")),
        P("group", "node"),
    )
    out_specs = P("node", "group")
    return jax.shard_map(shards, mesh=mesh, in_specs=in_specs, out_specs=out_specs, check_vma=False)
```

```python
import functools

import jax
import jax.numpy as jnp
from jax import lax
from jax.experimental import pallas as pl
from jax.experimental.pallas import tpu as pltpu
from jax.sharding import PartitionSpec as P

F = 1024
EXP_NODE = 2


def routed_shards(tokens, node_routes, combine, w_gate, w_up, w_down):
    node_count = lax.axis_size("node")
    tok_count = tokens.shape[0]
    col_width = tokens.shape[1]
    hid_dev = w_gate.shape[1]
    slots = 2 * tok_count * node_routes.shape[1] // node_count
    row_total = node_count * slots
    targets = jnp.arange(node_count, dtype=jnp.int32)
    node_hits = (node_routes[:, :, None] == targets[None, None, :]).astype(jnp.float32)
    member = jnp.sum(node_hits, axis=1)
    slot_rank = jnp.cumsum(member, axis=0) - member
    slot_numbers = jnp.arange(slots, dtype=jnp.float32)
    placed = member[:, :, None] * (slot_rank[:, :, None] == slot_numbers).astype(jnp.float32)
    pair_weights = combine.reshape(tok_count, -1, EXP_NODE).astype(jnp.float32) / 1024.0
    node_pair = jnp.einsum("tjm,tjk->tmk", node_hits, pair_weights)
    slot_weights = jnp.einsum("tmc,tmk->mck", placed, node_pair).astype(jnp.bfloat16)
    placed_low = placed.astype(jnp.bfloat16)
    send_rows = jnp.einsum(
        "tmc,td->mcd", placed_low, tokens, preferred_element_type=jnp.float32
    ).astype(jnp.bfloat16)
    send_rows = send_rows.reshape(node_count, slots * col_width)
    got_rows, got_weights = (
        lax.all_to_all(send_rows, "node", split_axis=0, concat_axis=0, tiled=True),
        lax.all_to_all(slot_weights, "node", split_axis=0, concat_axis=0, tiled=True),
    )
    node_rows = got_rows.reshape(row_total, col_width)
    weight_rows = got_weights.reshape(row_total, EXP_NODE).astype(jnp.float32)
    local_expert = lax.axis_index("group") * hid_dev // F
    expert_pick = (jnp.arange(EXP_NODE, dtype=jnp.int32) == local_expert).astype(jnp.float32)
    row_scale = jnp.sum(weight_rows * expert_pick[None, :], axis=1)
    whole_rows = lax.all_gather(node_rows, "group", axis=1, tiled=True)
    gate_acts = jnp.dot(whole_rows, w_gate, preferred_element_type=jnp.float32)
    up_acts = jnp.dot(whole_rows, w_up, preferred_element_type=jnp.float32)
    hidden = (row_scale[:, None] * jax.nn.silu(gate_acts) * up_acts).astype(jnp.bfloat16)
    contract = (((1,), (1,)), ((), ()))
    all_hidden = lax.all_gather(hidden, "group", axis=1, tiled=True)
    out_back = lax.dot_general(w_down, all_hidden, contract, preferred_element_type=jnp.float32)
    out_back = out_back.astype(jnp.bfloat16)
    returned = lax.all_to_all(out_back, "node", split_axis=1, concat_axis=1, tiled=True)
    mixed_out = lax.dot_general(
        placed_low.reshape(tok_count, row_total),
        returned,
        contract,
        preferred_element_type=jnp.float32,
    )
    return mixed_out.astype(jnp.bfloat16)


def pair_scales(node_routes, combine):
    node_count = lax.axis_size("node")
    targets = jnp.arange(node_count, dtype=jnp.int32)
    hits = (node_routes[:, :, None] == targets[None, None, :]).astype(jnp.float32)
    pairs = combine.reshape(combine.shape[0], -1, EXP_NODE).astype(jnp.float32) / 1024.0
    return jnp.einsum("tjm,tjk->tmk", hits, pairs).reshape(combine.shape[0], -1)


def fused_kernel(tok_in, scl_in, wg_hbm, wu_hbm, wd_hbm, out,
                 tok, scl, hid, part, inbox, wg, wu, wd, send, recv, local):
    groups = lax.axis_size("group")
    z, n = lax.axis_index("group"), lax.axis_index("node")
    core, x, y = n % 2, (n // 2) % 2, n // 4
    rows, width = tok_in.shape
    hid_dev = wg.shape[1]

    def partner(m):
        flip = lambda bit, on: 1 - bit if on else bit
        return (flip(y, m // 4 % 2) * 2 + flip(x, m // 2 % 2)) * 2 + flip(core, m % 2)

    own, chip_x, chip_y, chip_d = (partner(m) // 2 for m in (0, 2, 4, 6))
    ids, pending = {}, []

    def there(d):
        return None if d == 0 else jnp.logical_and(z + d >= 0, z + d < groups)

    def guarded(conds, body):
        conds = [c for c in conds if c is not None]
        if conds:
            pl.when(functools.reduce(jnp.logical_and, conds))(body)
        else:
            body()

    def describe(key, src, dst, node, group):
        i = ids.setdefault(key, len(ids))
        return pltpu.make_async_remote_copy(
            src_ref=src, dst_ref=dst, send_sem=send.at[i], recv_sem=recv.at[i],
            device_id=(node, group), device_id_type=pl.DeviceIdType.MESH)

    def push(key, ref, node, group=z, conds=(), dst=None):
        ref_to = ref if dst is None else dst
        make = lambda: describe(key, ref(), ref_to(), node, group)
        ids.setdefault(key, len(ids))
        guarded(conds, lambda: make().start())
        pending.append((conds, make))

    def arrive(key, ref, conds=()):
        ids.setdefault(key, len(ids))
        guarded(conds, lambda: describe(key, ref(), ref(), partner(1), z).wait_recv())

    loads = [pltpu.make_async_copy(a, b, local.at[i])
             for i, (a, b) in enumerate(((wg_hbm, wg), (wu_hbm, wu), (wd_hbm, wd)))]
    for load in loads:
        load.start()

    barrier = pltpu.get_barrier_semaphore()
    for m in range(1, 8):
        pl.semaphore_signal(barrier, inc=1, device_id=(partner(m), z), device_id_type=pl.DeviceIdType.MESH)
    for d in (-1, 1):
        guarded([there(d)], lambda d=d: pl.semaphore_signal(
            barrier, inc=1, device_id=(n, z + d), device_id_type=pl.DeviceIdType.MESH))
    tok[own, core, z] = tok_in[...]
    scl[own, core] = scl_in[...]
    pl.semaphore_wait(barrier, 7 + (z + 2) // 3 + (groups + 1 - z) // 3)

    def shard(chip, d):
        return lambda: tok.at[chip, core, z + d]

    half = rows // 2

    def half_shard(chip, d, which):
        return lambda: tok.at[chip, core, z + d, pl.ds(which * half, half)]

    def spread(d):
        for step in (-1, 1):
            if d * step <= 0:
                push(("t", step, abs(d)), shard(own, d), n, z + step, [c for c in (there(d), there(step)) if c is not None])
        conds = [there(d)] if d else []
        push(("x", d), shard(own, d), partner(2), conds=conds)
        push(("y", d), shard(own, d), partner(4), conds=conds)

    def turn(d):
        conds = [there(d)] if d else []
        arrive(("x", d), shard(chip_x, d), conds)
        push(("dy", d), half_shard(chip_x, d, 0), partner(4), conds=conds)
        arrive(("y", d), shard(chip_y, d), conds)
        push(("dx", d), half_shard(chip_y, d, 1), partner(2), conds=conds)

    spread(0)
    for m in range(1, 8):
        push(("scl", m), lambda: scl.at[own, core], partner(m))
    for r in range(1, groups):
        for d in (-r, r):
            arrive(("t", 1 if d < 0 else -1, r - 1), shard(own, d), [there(d)])
            spread(d)
        for d in ((0,) if r == 1 else (1 - r, r - 1)):
            turn(d)

    def column(chip, c):
        return lambda: tok.at[chip, c]

    def swap(k, chip):
        push(("sib", k), column(chip, core), partner(1))

    swap(0, own)

    def node_of(chip, c):
        return lambda: scl.at[chip, c]

    for load in loads:
        load.wait()
    for m in range(1, 8):
        arrive(("scl", m), node_of(partner(m) // 2, partner(m) % 2))
    expert = EXP_NODE * n + z * hid_dev // F
    lanes = scl.shape[-1]
    pick = (lax.broadcasted_iota(jnp.int32, (lanes, hid_dev), 0) == expert).astype(jnp.bfloat16)

    def make_hidden(k, chip):
        arrive(("sib", k), column(chip, 1 - core))
        scale = jnp.dot(scl[chip].reshape(2 * rows, lanes), pick, preferred_element_type=jnp.float32)
        gate = up = None
        for g in range(groups):
            block = tok[chip, :, g].reshape(2 * rows, width)
            depth = pl.ds(g * width, width)
            a = jnp.dot(block, wg[depth], preferred_element_type=jnp.float32)
            b = jnp.dot(block, wu[depth], preferred_element_type=jnp.float32)
            gate, up = (a, b) if g == 0 else (gate + a, up + b)
        hid[chip, z] = (scale * (gate / (1.0 + jnp.exp(-gate))) * up).astype(jnp.bfloat16)
        hop(k, chip, 0)

    def hop(k, chip, d):
        for step in (-1, 1):
            if d * step <= 0:
                push(("h", k, step, abs(d)), lambda: hid.at[chip, z + d], n, z + step,
                     [c for c in (there(d), there(step)) if c is not None])

    def relay(k, chip, r):
        for d in (-r, r):
            arrive(("h", k, 1 if d < 0 else -1, r - 1), lambda: hid.at[chip, z + d], [there(d)])
            hop(k, chip, d)

    def make_part(chip, ms):
        total = None
        for g in range(groups):
            term = lax.dot_general(hid[chip, g], wd[:, pl.ds(g * hid_dev, hid_dev)], (((1,), (1,)), ((), ())),
                                   preferred_element_type=jnp.float32)
            total = term if g == 0 else total + term
        part[chip] = total.astype(jnp.bfloat16).reshape(2, rows, width)
        for m in ms:
            push(("o", m), lambda m=m: part.at[chip, partner(m) % 2], partner(m), dst=lambda m=m: inbox.at[m])

    make_hidden(0, own)
    for d in (1 - groups, groups - 1):
        turn(d)
    swap(1, chip_x)
    swap(2, chip_y)
    relay(0, own, 1)
    make_hidden(1, chip_x)
    relay(0, own, 2)
    make_hidden(2, chip_y)
    relay(0, own, 3)
    relay(1, chip_x, 1)
    for d in [0] + [s * r for r in range(1, groups) for s in (-1, 1)]:
        conds = [there(d)] if d else []
        arrive(("dy", d), half_shard(chip_d, d, 0), conds)
        arrive(("dx", d), half_shard(chip_d, d, 1), conds)
    swap(3, chip_d)
    relay(1, chip_x, 2)
    relay(2, chip_y, 1)
    make_hidden(3, chip_d)
    relay(1, chip_x, 3)
    make_part(own, (1,))
    relay(2, chip_y, 2)
    relay(3, chip_d, 1)
    relay(2, chip_y, 3)
    make_part(chip_x, (2, 3))
    relay(3, chip_d, 2)
    make_part(chip_y, (4, 5))
    relay(3, chip_d, 3)
    make_part(chip_d, (6, 7))
    total = part[own, core].astype(jnp.float32)
    for m in range(1, 8):
        arrive(("o", m), lambda: inbox.at[m])
        total = total + inbox[m].astype(jnp.float32)
    out[...] = total.astype(jnp.bfloat16)
    for conds, make in pending:
        guarded(conds, lambda: make().wait_send())


def fused_shards(tokens, node_routes, combine, w_gate, w_up, w_down):
    rows, width = tokens.shape
    groups, nodes = lax.axis_size("group"), lax.axis_size("node")
    hid_dev = w_gate.shape[1]
    scales = pair_scales(node_routes, combine)
    scales = jnp.pad(scales, ((0, 0), (0, 128 - scales.shape[1]))).astype(jnp.bfloat16)
    vmem, hbm = pl.BlockSpec(memory_space=pltpu.VMEM), pl.BlockSpec(memory_space=pl.ANY)
    low = jnp.bfloat16
    return pl.pallas_call(
        fused_kernel,
        out_shape=jax.ShapeDtypeStruct((rows, width), low),
        in_specs=[vmem, vmem, hbm, hbm, hbm],
        out_specs=vmem,
        scratch_shapes=[
            pltpu.VMEM((nodes // 2, 2, groups, rows, width), low),
            pltpu.VMEM((nodes // 2, 2, rows, 128), low),
            pltpu.VMEM((nodes // 2, groups, 2 * rows, hid_dev), low),
            pltpu.VMEM((nodes // 2, 2, rows, width), low),
            pltpu.VMEM((nodes, rows, width), low),
            pltpu.VMEM(w_gate.shape, low),
            pltpu.VMEM(w_up.shape, low),
            pltpu.VMEM(w_down.shape, low),
            pltpu.SemaphoreType.DMA((96,)),
            pltpu.SemaphoreType.DMA((96,)),
            pltpu.SemaphoreType.DMA((3,)),
        ],
        compiler_params=pltpu.CompilerParams(
            collective_id=0, has_side_effects=True, vmem_limit_bytes=56 * 1024 * 1024),
    )(tokens, scales, w_gate, w_up, w_down)


def dense_shards(tokens, node_routes, combine, w_gate, w_up, w_down):
    hid_dev = w_gate.shape[1]
    scales = pair_scales(node_routes, combine).astype(jnp.bfloat16)
    all_scales = lax.all_gather(scales, "node", axis=0, tiled=True)
    column = lax.all_gather(tokens, "group", axis=1, tiled=True)
    rows = lax.all_gather(column, "node", axis=0, tiled=True)
    expert = EXP_NODE * lax.axis_index("node") + lax.axis_index("group") * hid_dev // F
    row_scale = lax.dynamic_slice_in_dim(all_scales, expert, 1, 1).astype(jnp.float32)
    gate_acts = jnp.dot(rows, w_gate, preferred_element_type=jnp.float32)
    up_acts = jnp.dot(rows, w_up, preferred_element_type=jnp.float32)
    hidden = (row_scale * jax.nn.silu(gate_acts) * up_acts).astype(jnp.bfloat16)
    all_hidden = lax.all_gather(hidden, "group", axis=1, tiled=True)
    contract = (((1,), (1,)), ((), ()))
    part = lax.dot_general(all_hidden, w_down, contract, preferred_element_type=jnp.float32)
    return lax.psum_scatter(part.astype(jnp.bfloat16), "node", scatter_dimension=0, tiled=True)


def shards(tokens, node_routes, *rest):
    slots = 2 * tokens.shape[0] * node_routes.shape[1] // lax.axis_size("node")
    if slots == tokens.shape[0] and lax.axis_size("node") == 8 and lax.axis_size("group") == 4:
        return fused_shards(tokens, node_routes, *rest)
    if slots == tokens.shape[0]:
        return dense_shards(tokens, node_routes, *rest)
    return routed_shards(tokens, node_routes, *rest)


def solution(mesh):
    in_specs = (
        P("node", "group"),
        P("node", None),
        P("node", None),
        P(None, ("node", "group")),
        P(None, ("node", "group")),
        P("group", "node"),
    )
    out_specs = P("node", "group")
    return jax.shard_map(shards, mesh=mesh, in_specs=in_specs, out_specs=out_specs, check_vma=False)
```

```python
import functools

import jax
import jax.numpy as jnp
from jax import lax
from jax.experimental import pallas as pl
from jax.experimental.pallas import tpu as pltpu
from jax.sharding import PartitionSpec as P

F = 1024
EXP_NODE = 2


def routed_shards(tokens, node_routes, combine, w_gate, w_up, w_down):
    node_count = lax.axis_size("node")
    tok_count = tokens.shape[0]
    col_width = tokens.shape[1]
    hid_dev = w_gate.shape[1]
    slots = 2 * tok_count * node_routes.shape[1] // node_count
    row_total = node_count * slots
    targets = jnp.arange(node_count, dtype=jnp.int32)
    node_hits = (node_routes[:, :, None] == targets[None, None, :]).astype(jnp.float32)
    member = jnp.sum(node_hits, axis=1)
    slot_rank = jnp.cumsum(member, axis=0) - member
    slot_numbers = jnp.arange(slots, dtype=jnp.float32)
    placed = member[:, :, None] * (slot_rank[:, :, None] == slot_numbers).astype(jnp.float32)
    pair_weights = combine.reshape(tok_count, -1, EXP_NODE).astype(jnp.float32) / 1024.0
    node_pair = jnp.einsum("tjm,tjk->tmk", node_hits, pair_weights)
    slot_weights = jnp.einsum("tmc,tmk->mck", placed, node_pair).astype(jnp.bfloat16)
    placed_low = placed.astype(jnp.bfloat16)
    send_rows = jnp.einsum(
        "tmc,td->mcd", placed_low, tokens, preferred_element_type=jnp.float32
    ).astype(jnp.bfloat16)
    send_rows = send_rows.reshape(node_count, slots * col_width)
    got_rows, got_weights = (
        lax.all_to_all(send_rows, "node", split_axis=0, concat_axis=0, tiled=True),
        lax.all_to_all(slot_weights, "node", split_axis=0, concat_axis=0, tiled=True),
    )
    node_rows = got_rows.reshape(row_total, col_width)
    weight_rows = got_weights.reshape(row_total, EXP_NODE).astype(jnp.float32)
    local_expert = lax.axis_index("group") * hid_dev // F
    expert_pick = (jnp.arange(EXP_NODE, dtype=jnp.int32) == local_expert).astype(jnp.float32)
    row_scale = jnp.sum(weight_rows * expert_pick[None, :], axis=1)
    whole_rows = lax.all_gather(node_rows, "group", axis=1, tiled=True)
    gate_acts = jnp.dot(whole_rows, w_gate, preferred_element_type=jnp.float32)
    up_acts = jnp.dot(whole_rows, w_up, preferred_element_type=jnp.float32)
    hidden = (row_scale[:, None] * jax.nn.silu(gate_acts) * up_acts).astype(jnp.bfloat16)
    contract = (((1,), (1,)), ((), ()))
    all_hidden = lax.all_gather(hidden, "group", axis=1, tiled=True)
    out_back = lax.dot_general(w_down, all_hidden, contract, preferred_element_type=jnp.float32)
    out_back = out_back.astype(jnp.bfloat16)
    returned = lax.all_to_all(out_back, "node", split_axis=1, concat_axis=1, tiled=True)
    mixed_out = lax.dot_general(
        placed_low.reshape(tok_count, row_total),
        returned,
        contract,
        preferred_element_type=jnp.float32,
    )
    return mixed_out.astype(jnp.bfloat16)


def pair_scales(node_routes, combine):
    node_count = lax.axis_size("node")
    targets = jnp.arange(node_count, dtype=jnp.int32)
    hits = (node_routes[:, :, None] == targets[None, None, :]).astype(jnp.float32)
    pairs = combine.reshape(combine.shape[0], -1, EXP_NODE).astype(jnp.float32) / 1024.0
    return jnp.einsum("tjm,tjk->tmk", hits, pairs).reshape(combine.shape[0], -1)


def fused_kernel(tok_in, scl_in, wg_hbm, wu_hbm, wd_hbm, out,
                 tok, scl, hid, part, inbox, wg, wu, wd, send, recv, local):
    groups = lax.axis_size("group")
    z, n = lax.axis_index("group"), lax.axis_index("node")
    core, x, y = n % 2, (n // 2) % 2, n // 4
    rows, width = tok_in.shape
    hid_dev = wg.shape[1]

    def partner(m):
        flip = lambda bit, on: 1 - bit if on else bit
        return (flip(y, m // 4 % 2) * 2 + flip(x, m // 2 % 2)) * 2 + flip(core, m % 2)

    own, chip_x, chip_y, chip_d = (partner(m) // 2 for m in (0, 2, 4, 6))
    ids, pending = {}, []

    def there(d):
        return None if d == 0 else jnp.logical_and(z + d >= 0, z + d < groups)

    def guarded(conds, body):
        conds = [c for c in conds if c is not None]
        if conds:
            pl.when(functools.reduce(jnp.logical_and, conds))(body)
        else:
            body()

    def describe(key, src, dst, node, group):
        i = ids.setdefault(key, len(ids))
        return pltpu.make_async_remote_copy(
            src_ref=src, dst_ref=dst, send_sem=send.at[i], recv_sem=recv.at[i],
            device_id=(node, group), device_id_type=pl.DeviceIdType.MESH)

    def push(key, ref, node, group=z, conds=(), dst=None):
        ref_to = ref if dst is None else dst
        make = lambda: describe(key, ref(), ref_to(), node, group)
        ids.setdefault(key, len(ids))
        guarded(conds, lambda: make().start())
        pending.append((conds, make))

    def arrive(key, ref, conds=()):
        ids.setdefault(key, len(ids))
        guarded(conds, lambda: describe(key, ref(), ref(), partner(1), z).wait_recv())

    loads = [pltpu.make_async_copy(a, b, local.at[i])
             for i, (a, b) in enumerate(((wg_hbm, wg), (wu_hbm, wu), (wd_hbm, wd)))]
    for load in loads:
        load.start()

    barrier = pltpu.get_barrier_semaphore()
    for m in range(1, 8):
        pl.semaphore_signal(barrier, inc=1, device_id=(partner(m), z), device_id_type=pl.DeviceIdType.MESH)
    for d in (-1, 1):
        guarded([there(d)], lambda d=d: pl.semaphore_signal(
            barrier, inc=1, device_id=(n, z + d), device_id_type=pl.DeviceIdType.MESH))
    tok[own, core, z] = tok_in[...]
    scl[own, core] = scl_in[...]
    pl.semaphore_wait(barrier, 7 + (z + 2) // 3 + (groups + 1 - z) // 3)

    def shard(chip, d):
        return lambda: tok.at[chip, core, z + d]

    half = rows // 2

    def half_shard(chip, d, which):
        return lambda: tok.at[chip, core, z + d, pl.ds(which * half, half)]

    def spread(d):
        for step in (-1, 1):
            if d * step <= 0:
                push(("t", step, abs(d)), shard(own, d), n, z + step, [c for c in (there(d), there(step)) if c is not None])
        conds = [there(d)] if d else []
        push(("x", d), shard(own, d), partner(2), conds=conds)
        push(("y", d), shard(own, d), partner(4), conds=conds)

    def turn(d):
        conds = [there(d)] if d else []
        arrive(("x", d), shard(chip_x, d), conds)
        push(("dy", d), half_shard(chip_x, d, 0), partner(4), conds=conds)
        arrive(("y", d), shard(chip_y, d), conds)
        push(("dx", d), half_shard(chip_y, d, 1), partner(2), conds=conds)

    spread(0)
    for m in range(1, 8):
        push(("scl", m), lambda: scl.at[own, core], partner(m))
    for r in range(1, groups):
        for d in (-r, r):
            arrive(("t", 1 if d < 0 else -1, r - 1), shard(own, d), [there(d)])
            spread(d)
        for d in ((0,) if r == 1 else (1 - r, r - 1)):
            turn(d)

    def column(chip, c):
        return lambda: tok.at[chip, c]

    def swap(k, chip):
        push(("sib", k), column(chip, core), partner(1))

    swap(0, own)

    def node_of(chip, c):
        return lambda: scl.at[chip, c]

    for load in loads:
        load.wait()
    for m in range(1, 8):
        arrive(("scl", m), node_of(partner(m) // 2, partner(m) % 2))
    expert = EXP_NODE * n + z * hid_dev // F
    lanes = scl.shape[-1]
    pick = (lax.broadcasted_iota(jnp.int32, (lanes, hid_dev), 0) == expert).astype(jnp.bfloat16)

    def make_hidden(k, chip, first, count):
        if k < 4:
            arrive(("sib", k), column(chip, 1 - core))
        cores = pl.ds(first, count)
        scale = jnp.dot(scl[chip, cores].reshape(count * rows, lanes), pick, preferred_element_type=jnp.float32)
        gate = up = None
        for g in range(groups):
            block = tok[chip, cores, g].reshape(count * rows, width)
            depth = pl.ds(g * width, width)
            a = jnp.dot(block, wg[depth], preferred_element_type=jnp.float32)
            b = jnp.dot(block, wu[depth], preferred_element_type=jnp.float32)
            gate, up = (a, b) if g == 0 else (gate + a, up + b)
        chunk = pl.ds(first * rows, count * rows)
        hid[chip, z, chunk] = (scale * (gate / (1.0 + jnp.exp(-gate))) * up).astype(jnp.bfloat16)
        hop((k, chip, first, count), 0)

    def hop(piece, d):
        k, chip, first, count = piece
        for step in (-1, 1):
            if d * step <= 0:
                push(("h", k, step, abs(d)),
                     lambda: hid.at[chip, z + d, pl.ds(first * rows, count * rows)], n, z + step,
                     [c for c in (there(d), there(step)) if c is not None])

    def relay(piece, r):
        k, chip, first, count = piece
        for d in (-r, r):
            arrive(("h", k, 1 if d < 0 else -1, r - 1),
                   lambda: hid.at[chip, z + d, pl.ds(first * rows, count * rows)], [there(d)])
            hop(piece, d)

    def make_part(piece, ms):
        k, chip, first, count = piece
        total = None
        for g in range(groups):
            term = lax.dot_general(hid[chip, g, pl.ds(first * rows, count * rows)],
                                   wd[:, pl.ds(g * hid_dev, hid_dev)], (((1,), (1,)), ((), ())),
                                   preferred_element_type=jnp.float32)
            total = term if g == 0 else total + term
        part[chip, pl.ds(first, count)] = total.astype(jnp.bfloat16).reshape(count, rows, width)
        for m in ms:
            conds = [core != first] if m == 1 else []
            push(("o", m), lambda m=m: part.at[chip, partner(m) % 2], partner(m), conds=conds,
                 dst=lambda m=m: inbox.at[m])

    own_a, col_x, col_y, col_d, own_b = (
        (0, own, 0, 1), (1, chip_x, 0, 2), (2, chip_y, 0, 2), (3, chip_d, 0, 2), (4, own, 1, 1))

    def diagonal():
        for d in [0] + [s * r for r in range(1, groups) for s in (-1, 1)]:
            conds = [there(d)] if d else []
            arrive(("dy", d), half_shard(chip_d, d, 0), conds)
            arrive(("dx", d), half_shard(chip_d, d, 1), conds)
        swap(3, chip_d)

    make_hidden(*own_a)
    for d in (1 - groups, groups - 1):
        turn(d)
    swap(1, chip_x)
    swap(2, chip_y)
    make_hidden(*col_x)
    make_hidden(*col_y)
    relay(own_a, 1)
    relay(own_a, 2)
    relay(own_a, 3)
    relay(col_x, 1)
    relay(col_x, 2)
    relay(col_x, 3)
    diagonal()
    make_hidden(*col_d)
    relay(col_y, 1)
    make_hidden(*own_b)
    relay(col_y, 2)
    relay(col_y, 3)
    make_part(own_a, (1,))
    make_part(col_x, (2, 3))
    relay(col_d, 1)
    relay(col_d, 2)
    make_part(col_y, (4, 5))
    relay(col_d, 3)
    relay(own_b, 1)
    relay(own_b, 2)
    make_part(col_d, (6, 7))
    relay(own_b, 3)
    make_part(own_b, (1,))
    total = part[own, core].astype(jnp.float32)
    for m in range(1, 8):
        arrive(("o", m), lambda: inbox.at[m])
        total = total + inbox[m].astype(jnp.float32)
    out[...] = total.astype(jnp.bfloat16)
    for conds, make in pending:
        guarded(conds, lambda: make().wait_send())


def fused_shards(tokens, node_routes, combine, w_gate, w_up, w_down):
    rows, width = tokens.shape
    groups, nodes = lax.axis_size("group"), lax.axis_size("node")
    hid_dev = w_gate.shape[1]
    scales = pair_scales(node_routes, combine)
    scales = jnp.pad(scales, ((0, 0), (0, 128 - scales.shape[1]))).astype(jnp.bfloat16)
    vmem, hbm = pl.BlockSpec(memory_space=pltpu.VMEM), pl.BlockSpec(memory_space=pl.ANY)
    low = jnp.bfloat16
    return pl.pallas_call(
        fused_kernel,
        out_shape=jax.ShapeDtypeStruct((rows, width), low),
        in_specs=[vmem, vmem, hbm, hbm, hbm],
        out_specs=vmem,
        scratch_shapes=[
            pltpu.VMEM((nodes // 2, 2, groups, rows, width), low),
            pltpu.VMEM((nodes // 2, 2, rows, 128), low),
            pltpu.VMEM((nodes // 2, groups, 2 * rows, hid_dev), low),
            pltpu.VMEM((nodes // 2, 2, rows, width), low),
            pltpu.VMEM((nodes, rows, width), low),
            pltpu.VMEM(w_gate.shape, low),
            pltpu.VMEM(w_up.shape, low),
            pltpu.VMEM(w_down.shape, low),
            pltpu.SemaphoreType.DMA((96,)),
            pltpu.SemaphoreType.DMA((96,)),
            pltpu.SemaphoreType.DMA((3,)),
        ],
        compiler_params=pltpu.CompilerParams(
            collective_id=0, has_side_effects=True, vmem_limit_bytes=56 * 1024 * 1024),
    )(tokens, scales, w_gate, w_up, w_down)


def dense_shards(tokens, node_routes, combine, w_gate, w_up, w_down):
    hid_dev = w_gate.shape[1]
    scales = pair_scales(node_routes, combine).astype(jnp.bfloat16)
    all_scales = lax.all_gather(scales, "node", axis=0, tiled=True)
    column = lax.all_gather(tokens, "group", axis=1, tiled=True)
    rows = lax.all_gather(column, "node", axis=0, tiled=True)
    expert = EXP_NODE * lax.axis_index("node") + lax.axis_index("group") * hid_dev // F
    row_scale = lax.dynamic_slice_in_dim(all_scales, expert, 1, 1).astype(jnp.float32)
    gate_acts = jnp.dot(rows, w_gate, preferred_element_type=jnp.float32)
    up_acts = jnp.dot(rows, w_up, preferred_element_type=jnp.float32)
    hidden = (row_scale * jax.nn.silu(gate_acts) * up_acts).astype(jnp.bfloat16)
    all_hidden = lax.all_gather(hidden, "group", axis=1, tiled=True)
    contract = (((1,), (1,)), ((), ()))
    part = lax.dot_general(all_hidden, w_down, contract, preferred_element_type=jnp.float32)
    return lax.psum_scatter(part.astype(jnp.bfloat16), "node", scatter_dimension=0, tiled=True)


def shards(tokens, node_routes, *rest):
    slots = 2 * tokens.shape[0] * node_routes.shape[1] // lax.axis_size("node")
    if slots == tokens.shape[0] and lax.axis_size("node") == 8 and lax.axis_size("group") == 4:
        return fused_shards(tokens, node_routes, *rest)
    if slots == tokens.shape[0]:
        return dense_shards(tokens, node_routes, *rest)
    return routed_shards(tokens, node_routes, *rest)


def solution(mesh):
    in_specs = (
        P("node", "group"),
        P("node", None),
        P("node", None),
        P(None, ("node", "group")),
        P(None, ("node", "group")),
        P("group", "node"),
    )
    out_specs = P("node", "group")
    return jax.shard_map(shards, mesh=mesh, in_specs=in_specs, out_specs=out_specs, check_vma=False)
```

```python
import functools

import jax
import jax.numpy as jnp
from jax import lax
from jax.experimental import pallas as pl
from jax.experimental.pallas import tpu as pltpu
from jax.sharding import PartitionSpec as P

F = 1024
EXP_NODE = 2


def routed_shards(tokens, node_routes, combine, w_gate, w_up, w_down):
    node_count = lax.axis_size("node")
    tok_count = tokens.shape[0]
    col_width = tokens.shape[1]
    hid_dev = w_gate.shape[1]
    slots = 2 * tok_count * node_routes.shape[1] // node_count
    row_total = node_count * slots
    targets = jnp.arange(node_count, dtype=jnp.int32)
    node_hits = (node_routes[:, :, None] == targets[None, None, :]).astype(jnp.float32)
    member = jnp.sum(node_hits, axis=1)
    slot_rank = jnp.cumsum(member, axis=0) - member
    slot_numbers = jnp.arange(slots, dtype=jnp.float32)
    placed = member[:, :, None] * (slot_rank[:, :, None] == slot_numbers).astype(jnp.float32)
    pair_weights = combine.reshape(tok_count, -1, EXP_NODE).astype(jnp.float32) / 1024.0
    node_pair = jnp.einsum("tjm,tjk->tmk", node_hits, pair_weights)
    slot_weights = jnp.einsum("tmc,tmk->mck", placed, node_pair).astype(jnp.bfloat16)
    placed_low = placed.astype(jnp.bfloat16)
    send_rows = jnp.einsum(
        "tmc,td->mcd", placed_low, tokens, preferred_element_type=jnp.float32
    ).astype(jnp.bfloat16)
    send_rows = send_rows.reshape(node_count, slots * col_width)
    got_rows, got_weights = (
        lax.all_to_all(send_rows, "node", split_axis=0, concat_axis=0, tiled=True),
        lax.all_to_all(slot_weights, "node", split_axis=0, concat_axis=0, tiled=True),
    )
    node_rows = got_rows.reshape(row_total, col_width)
    weight_rows = got_weights.reshape(row_total, EXP_NODE).astype(jnp.float32)
    local_expert = lax.axis_index("group") * hid_dev // F
    expert_pick = (jnp.arange(EXP_NODE, dtype=jnp.int32) == local_expert).astype(jnp.float32)
    row_scale = jnp.sum(weight_rows * expert_pick[None, :], axis=1)
    whole_rows = lax.all_gather(node_rows, "group", axis=1, tiled=True)
    gate_acts = jnp.dot(whole_rows, w_gate, preferred_element_type=jnp.float32)
    up_acts = jnp.dot(whole_rows, w_up, preferred_element_type=jnp.float32)
    hidden = (row_scale[:, None] * jax.nn.silu(gate_acts) * up_acts).astype(jnp.bfloat16)
    contract = (((1,), (1,)), ((), ()))
    all_hidden = lax.all_gather(hidden, "group", axis=1, tiled=True)
    out_back = lax.dot_general(w_down, all_hidden, contract, preferred_element_type=jnp.float32)
    out_back = out_back.astype(jnp.bfloat16)
    returned = lax.all_to_all(out_back, "node", split_axis=1, concat_axis=1, tiled=True)
    mixed_out = lax.dot_general(
        placed_low.reshape(tok_count, row_total),
        returned,
        contract,
        preferred_element_type=jnp.float32,
    )
    return mixed_out.astype(jnp.bfloat16)


def pair_scales(node_routes, combine):
    node_count = lax.axis_size("node")
    targets = jnp.arange(node_count, dtype=jnp.int32)
    hits = (node_routes[:, :, None] == targets[None, None, :]).astype(jnp.float32)
    pairs = combine.reshape(combine.shape[0], -1, EXP_NODE).astype(jnp.float32) / 1024.0
    return jnp.einsum("tjm,tjk->tmk", hits, pairs).reshape(combine.shape[0], -1)


def fused_kernel(tok_in, scl_in, wg_hbm, wu_hbm, wd_hbm, out,
                 tok, scl, hid, part, inbox, wg, wu, wd, send, recv, local):
    groups = lax.axis_size("group")
    z, n = lax.axis_index("group"), lax.axis_index("node")
    core, x, y = n % 2, (n // 2) % 2, n // 4
    rows, width = tok_in.shape
    hid_dev = wg.shape[1]

    def partner(m):
        flip = lambda bit, on: 1 - bit if on else bit
        return (flip(y, m // 4 % 2) * 2 + flip(x, m // 2 % 2)) * 2 + flip(core, m % 2)

    own, chip_x, chip_y, chip_d = (partner(m) // 2 for m in (0, 2, 4, 6))
    ids, pending = {}, []

    def there(d):
        return None if d == 0 else jnp.logical_and(z + d >= 0, z + d < groups)

    def guarded(conds, body):
        conds = [c for c in conds if c is not None]
        if conds:
            pl.when(functools.reduce(jnp.logical_and, conds))(body)
        else:
            body()

    def describe(key, src, dst, node, group):
        i = ids.setdefault(key, len(ids))
        return pltpu.make_async_remote_copy(
            src_ref=src, dst_ref=dst, send_sem=send.at[i], recv_sem=recv.at[i],
            device_id=(node, group), device_id_type=pl.DeviceIdType.MESH)

    def push(key, ref, node, group=z, conds=(), dst=None):
        ref_to = ref if dst is None else dst
        make = lambda: describe(key, ref(), ref_to(), node, group)
        ids.setdefault(key, len(ids))
        guarded(conds, lambda: make().start())
        pending.append((conds, make))

    def arrive(key, ref, conds=()):
        ids.setdefault(key, len(ids))
        guarded(conds, lambda: describe(key, ref(), ref(), partner(1), z).wait_recv())

    loads = [pltpu.make_async_copy(a, b, local.at[i])
             for i, (a, b) in enumerate(((wg_hbm, wg), (wu_hbm, wu), (wd_hbm, wd)))]
    for load in loads:
        load.start()

    barrier = pltpu.get_barrier_semaphore()
    for m in range(1, 8):
        pl.semaphore_signal(barrier, inc=1, device_id=(partner(m), z), device_id_type=pl.DeviceIdType.MESH)
    for d in (-1, 1):
        guarded([there(d)], lambda d=d: pl.semaphore_signal(
            barrier, inc=1, device_id=(n, z + d), device_id_type=pl.DeviceIdType.MESH))
    tok[own, core, z] = tok_in[...]
    scl[own, core] = scl_in[...]
    pl.semaphore_wait(barrier, 7 + (z + 2) // 3 + (groups + 1 - z) // 3)

    def shard(chip, d):
        return lambda: tok.at[chip, core, z + d]

    half = rows // 2

    def half_shard(chip, d, which):
        return lambda: tok.at[chip, core, z + d, pl.ds(which * half, half)]

    def spread(d):
        for step in (-1, 1):
            if d * step <= 0:
                push(("t", step, abs(d)), shard(own, d), n, z + step, [c for c in (there(d), there(step)) if c is not None])
        conds = [there(d)] if d else []
        push(("x", d), shard(own, d), partner(2), conds=conds)
        push(("y", d), shard(own, d), partner(4), conds=conds)

    def turn(d):
        conds = [there(d)] if d else []
        arrive(("x", d), shard(chip_x, d), conds)
        push(("dy", d), half_shard(chip_x, d, 0), partner(4), conds=conds)
        arrive(("y", d), shard(chip_y, d), conds)
        push(("dx", d), half_shard(chip_y, d, 1), partner(2), conds=conds)

    spread(0)
    for m in range(1, 8):
        push(("scl", m), lambda: scl.at[own, core], partner(m))
    for r in range(1, groups):
        for d in (-r, r):
            arrive(("t", 1 if d < 0 else -1, r - 1), shard(own, d), [there(d)])
            spread(d)
        for d in ((0,) if r == 1 else (1 - r, r - 1)):
            turn(d)

    def column(chip, c):
        return lambda: tok.at[chip, c]

    def swap(k, chip):
        push(("sib", k), column(chip, core), partner(1))

    swap(0, own)

    def node_of(chip, c):
        return lambda: scl.at[chip, c]

    for load in loads:
        load.wait()
    for m in range(1, 8):
        arrive(("scl", m), node_of(partner(m) // 2, partner(m) % 2))
    expert = EXP_NODE * n + z * hid_dev // F
    lanes = scl.shape[-1]
    pick = (lax.broadcasted_iota(jnp.int32, (lanes, hid_dev), 0) == expert).astype(jnp.bfloat16)

    def make_hidden(k, chip, first, count):
        if k < 4:
            arrive(("sib", k), column(chip, 1 - core))
        cores = pl.ds(first, count)
        scale = jnp.dot(scl[chip, cores].reshape(count * rows, lanes), pick, preferred_element_type=jnp.float32)
        gate = up = None
        for g in range(groups):
            block = tok[chip, cores, g].reshape(count * rows, width)
            depth = pl.ds(g * width, width)
            a = jnp.dot(block, wg[depth], preferred_element_type=jnp.float32)
            b = jnp.dot(block, wu[depth], preferred_element_type=jnp.float32)
            gate, up = (a, b) if g == 0 else (gate + a, up + b)
        chunk = pl.ds(first * rows, count * rows)
        hid[chip, z, chunk] = (scale * (gate / (1.0 + jnp.exp(-gate))) * up).astype(jnp.bfloat16)
        hop((k, chip, first, count), 0)

    def hop(piece, d):
        k, chip, first, count = piece
        for step in (-1, 1):
            if d * step <= 0:
                push(("h", k, step, abs(d)),
                     lambda: hid.at[chip, z + d, pl.ds(first * rows, count * rows)], n, z + step,
                     [c for c in (there(d), there(step)) if c is not None])

    def relay(piece, r):
        k, chip, first, count = piece
        for d in (-r, r):
            arrive(("h", k, 1 if d < 0 else -1, r - 1),
                   lambda: hid.at[chip, z + d, pl.ds(first * rows, count * rows)], [there(d)])
            hop(piece, d)

    def make_part(piece, ms):
        k, chip, first, count = piece
        total = None
        for g in range(groups):
            term = lax.dot_general(hid[chip, g, pl.ds(first * rows, count * rows)],
                                   wd[:, pl.ds(g * hid_dev, hid_dev)], (((1,), (1,)), ((), ())),
                                   preferred_element_type=jnp.float32)
            total = term if g == 0 else total + term
        part[chip, pl.ds(first, count)] = total.astype(jnp.bfloat16).reshape(count, rows, width)
        for m in ms:
            conds = []
            if count == 1:
                conds = [core == first if m % 2 == 0 else core != first]
            push(("o", m), lambda m=m: part.at[chip, partner(m) % 2], partner(m), conds=conds,
                 dst=lambda m=m: inbox.at[m])

    own_a, col_x, col_y, dia_a, own_b, dia_b = (
        (0, own, 0, 1), (1, chip_x, 0, 2), (2, chip_y, 0, 2), (3, chip_d, 0, 1), (4, own, 1, 1), (5, chip_d, 1, 1))

    def diagonal():
        for d in [0] + [s * r for r in range(1, groups) for s in (-1, 1)]:
            conds = [there(d)] if d else []
            arrive(("dy", d), half_shard(chip_d, d, 0), conds)
            arrive(("dx", d), half_shard(chip_d, d, 1), conds)
        swap(3, chip_d)

    make_hidden(*own_a)
    make_hidden(*own_b)
    for d in (1 - groups, groups - 1):
        turn(d)
    swap(1, chip_x)
    swap(2, chip_y)
    relay(own_a, 1)
    make_hidden(*col_x)
    make_hidden(*col_y)
    relay(own_a, 2)
    relay(own_a, 3)
    relay(own_b, 1)
    relay(own_b, 2)
    relay(own_b, 3)
    diagonal()
    make_hidden(*dia_a)
    make_hidden(*dia_b)
    relay(col_x, 1)
    relay(col_x, 2)
    relay(col_x, 3)
    make_part(own_a, (1,))
    make_part(own_b, (1,))
    relay(col_y, 1)
    make_part(col_x, (2, 3))
    relay(col_y, 2)
    relay(col_y, 3)
    relay(dia_a, 1)
    relay(dia_a, 2)
    make_part(col_y, (4, 5))
    relay(dia_a, 3)
    relay(dia_b, 1)
    relay(dia_b, 2)
    make_part(dia_a, (6, 7))
    relay(dia_b, 3)
    make_part(dia_b, (6, 7))
    total = part[own, core].astype(jnp.float32)
    for m in range(1, 8):
        arrive(("o", m), lambda: inbox.at[m])
        total = total + inbox[m].astype(jnp.float32)
    out[...] = total.astype(jnp.bfloat16)
    for conds, make in pending:
        guarded(conds, lambda: make().wait_send())


def fused_shards(tokens, node_routes, combine, w_gate, w_up, w_down):
    rows, width = tokens.shape
    groups, nodes = lax.axis_size("group"), lax.axis_size("node")
    hid_dev = w_gate.shape[1]
    scales = pair_scales(node_routes, combine)
    scales = jnp.pad(scales, ((0, 0), (0, 128 - scales.shape[1]))).astype(jnp.bfloat16)
    vmem, hbm = pl.BlockSpec(memory_space=pltpu.VMEM), pl.BlockSpec(memory_space=pl.ANY)
    low = jnp.bfloat16
    return pl.pallas_call(
        fused_kernel,
        out_shape=jax.ShapeDtypeStruct((rows, width), low),
        in_specs=[vmem, vmem, hbm, hbm, hbm],
        out_specs=vmem,
        scratch_shapes=[
            pltpu.VMEM((nodes // 2, 2, groups, rows, width), low),
            pltpu.VMEM((nodes // 2, 2, rows, 128), low),
            pltpu.VMEM((nodes // 2, groups, 2 * rows, hid_dev), low),
            pltpu.VMEM((nodes // 2, 2, rows, width), low),
            pltpu.VMEM((nodes, rows, width), low),
            pltpu.VMEM(w_gate.shape, low),
            pltpu.VMEM(w_up.shape, low),
            pltpu.VMEM(w_down.shape, low),
            pltpu.SemaphoreType.DMA((128,)),
            pltpu.SemaphoreType.DMA((128,)),
            pltpu.SemaphoreType.DMA((3,)),
        ],
        compiler_params=pltpu.CompilerParams(
            collective_id=0, has_side_effects=True, vmem_limit_bytes=56 * 1024 * 1024),
    )(tokens, scales, w_gate, w_up, w_down)


def dense_shards(tokens, node_routes, combine, w_gate, w_up, w_down):
    hid_dev = w_gate.shape[1]
    scales = pair_scales(node_routes, combine).astype(jnp.bfloat16)
    all_scales = lax.all_gather(scales, "node", axis=0, tiled=True)
    column = lax.all_gather(tokens, "group", axis=1, tiled=True)
    rows = lax.all_gather(column, "node", axis=0, tiled=True)
    expert = EXP_NODE * lax.axis_index("node") + lax.axis_index("group") * hid_dev // F
    row_scale = lax.dynamic_slice_in_dim(all_scales, expert, 1, 1).astype(jnp.float32)
    gate_acts = jnp.dot(rows, w_gate, preferred_element_type=jnp.float32)
    up_acts = jnp.dot(rows, w_up, preferred_element_type=jnp.float32)
    hidden = (row_scale * jax.nn.silu(gate_acts) * up_acts).astype(jnp.bfloat16)
    all_hidden = lax.all_gather(hidden, "group", axis=1, tiled=True)
    contract = (((1,), (1,)), ((), ()))
    part = lax.dot_general(all_hidden, w_down, contract, preferred_element_type=jnp.float32)
    return lax.psum_scatter(part.astype(jnp.bfloat16), "node", scatter_dimension=0, tiled=True)


def shards(tokens, node_routes, *rest):
    slots = 2 * tokens.shape[0] * node_routes.shape[1] // lax.axis_size("node")
    if slots == tokens.shape[0] and lax.axis_size("node") == 8 and lax.axis_size("group") == 4:
        return fused_shards(tokens, node_routes, *rest)
    if slots == tokens.shape[0]:
        return dense_shards(tokens, node_routes, *rest)
    return routed_shards(tokens, node_routes, *rest)


def solution(mesh):
    in_specs = (
        P("node", "group"),
        P("node", None),
        P("node", None),
        P(None, ("node", "group")),
        P(None, ("node", "group")),
        P("group", "node"),
    )
    out_specs = P("node", "group")
    return jax.shard_map(shards, mesh=mesh, in_specs=in_specs, out_specs=out_specs, check_vma=False)
```
